256 devices in a mesh: dp: 16 (over z, x_lo), tensor: 16 (over y, x_hi, core).
Axes of the slice: x: 4 (x_hi: 2, x_lo: 2; x = x_hi * 2 + x_lo), y: 4, z: 8, core: 2. Of those that a mesh axis runs over, the one named last changes fastest.
Arguments:
- hidden: bfloat16 [2048, 28672], P('dp', 'tensor'), may hold values from -0.1875 to 0.1875
- out_grad: bfloat16 [2048, 8192], P('tensor', 'dp'), may hold values from -8 to 8
- down_weight: bfloat16 [28672, 8192], P('tensor', 'dp'), may hold values from -0.03125 to 0.03125
- clip_mask: int32 [2048, 28672], P('dp', 'tensor'), may hold values 0 or 1
Outputs:
- grad_hidden: bfloat16 [2048, 28672], P('dp', 'tensor')
- weight_grad: bfloat16 [28672, 8192], P('tensor', 'dp')
The draws below stay inside these ranges and needn't reach their ends.
All inputs are finite; a program needn't handle non-finite values. No bound on the sum of `clip_mask` on one device may be relied on, other than what follows from the above.
Results may differ from the reference program's by a relative error of at most 0.028.
Values may be sent and summed in bfloat16 or wider, within the bound.
No kernel may reach another device: no remote copies, remote signals or barrier semaphores. Data moves between devices by JAX's collectives and lax.ppermute only.
A program may use at most 128 MiB of HBM per device.

```python
import math
import jax
import jax.numpy as jnp
import numpy as np
from jax import lax

D = 8192
FF = 28672
TOKENS = 2048
BLOCKS = 16
LOCAL = 1792
INNER = 64
COLS = 512
N_DP = 16


def set_ends(values, rng, low, largest):
    index_at = [jax.random.randint(jax.random.fold_in(rng, axis), (), 0, length) for axis, length in enumerate(values.shape)]
    longest = values.shape.index(max(values.shape))
    next_to = index_at[:longest] + [(index_at[longest] + 1) % values.shape[longest]] + index_at[longest + 1:]
    return values.at[tuple(index_at)].set(low).at[tuple(next_to)].set(largest)


def shard_levels(own_key, dims, cuts, low, largest):
    factor_of = 1.0
    for dim, parts in cuts:
        draws = jax.random.uniform(jax.random.fold_in(jax.random.fold_in(own_key, 6), dim), (parts,), jnp.float32, low / len(cuts), largest / len(cuts))
        factor_of = factor_of * jnp.repeat(jnp.exp(draws), dims[dim] // parts).reshape((-1,) + (1,) * (len(dims) - 1 - dim))
    return factor_of


def bell_draw(own_key, shape, scale, reach, split=(), dtype=jnp.bfloat16):
    entries = jax.random.normal(own_key, shape, jnp.float32) * scale
    if len(split) > 0:
        entries = shard_levels(own_key, shape, split, -0.22, 0.18) * entries
    return jnp.clip(entries, min=-reach, max=reach).astype(dtype)


def setup_inputs(seed: int = 0) -> dict:
    seeds = jax.random.split(jax.random.key(seed), 5)
    return {
        "hidden": bell_draw(seeds[0], (TOKENS, FF), 0.03, 0.1875, ((0, 16), (1, 16))),
        "out_grad": bell_draw(seeds[1], (TOKENS, D), 1.5, 8.0, ((0, 16), (1, 16))),
        "down_weight": bell_draw(seeds[2], (FF, D), FF ** -0.5, 0.03125, ((0, 16), (1, 16))),
        "clip_mask": set_ends((jax.random.randint(seeds[3], (TOKENS, FF), 0, 8) < 7).astype(jnp.int32), jax.random.fold_in(seeds[3], 1), 0, 1),
    }


def paley_table():
    modulus = 13
    residues = set((number * number % modulus for number in range(1, modulus)))
    character = np.zeros(modulus)
    for number in range(1, modulus):
        character[number] = 1.0 if number in residues else -1.0
    conference = np.zeros((modulus + 1, modulus + 1))
    conference[0, 1:] = 1.0
    conference[1:, 0] = 1.0
    for row_index in range(modulus):
        for col_index in range(modulus):
            conference[row_index + 1, col_index + 1] = character[(col_index - row_index) % modulus]
    block_sign = np.array([[1.0, -1.0], [-1.0, -1.0]])
    block_diag = np.array([[1.0, 1.0], [1.0, -1.0]])
    return np.kron(conference, block_sign) + np.kron(np.eye(modulus + 1), block_diag)

def sylvester(target_order):
    matrix = np.ones((1, 1))
    doubler = np.array([[1.0, 1.0], [1.0, -1.0]])
    while matrix.shape[0] < target_order:
        matrix = np.kron(doubler, matrix)
    return matrix

def local_rotate(values):
    row_count = values.shape[0]
    paley = jnp.asarray(paley_table(), jnp.float32)
    inner_table = jnp.asarray(sylvester(INNER), jnp.float32)
    shaped = values.astype(jnp.float32).reshape(row_count, BLOCKS, 28, INNER)
    shaped = jnp.einsum('tcae,ab->tcbe', shaped, paley, precision=lax.Precision.HIGHEST)
    shaped = jnp.einsum('tcae,ef->tcaf', shaped, inner_table, precision=lax.Precision.HIGHEST)
    return lax.optimization_barrier((shaped.reshape(row_count, FF) / math.sqrt(FF)).astype(jnp.bfloat16))

def cross_rotate(values):
    row_count = values.shape[0]
    sign_table = jnp.asarray(sylvester(BLOCKS), jnp.float32)
    shaped = values.astype(jnp.float32).reshape(row_count, BLOCKS, LOCAL)
    mixed = jnp.einsum('tcj,cd->tdj', shaped, sign_table, precision=lax.Precision.HIGHEST)
    return mixed.reshape(row_count, FF).astype(jnp.bfloat16)

def reference(hidden, out_grad, down_weight, clip_mask):
    turned_hidden = local_rotate(hidden)
    rotated = cross_rotate(turned_hidden)
    grad_inter = jnp.zeros((TOKENS, FF), jnp.float32)
    for block_index in range(N_DP):
        low = block_index * COLS
        partial_term = jnp.dot(out_grad[:, low:low + COLS], down_weight[:, low:low + COLS].T, preferred_element_type=jnp.float32)
        grad_inter = grad_inter + lax.optimization_barrier(partial_term.astype(jnp.bfloat16)).astype(jnp.float32)
    masked = jnp.where(clip_mask > 0, grad_inter, jnp.zeros_like(grad_inter)).astype(jnp.bfloat16)
    turned_grad = local_rotate(masked)
    grad_hidden = cross_rotate(turned_grad)
    weight_grad = jnp.dot(rotated.T, out_grad, preferred_element_type=jnp.float32).astype(jnp.bfloat16)
    return (grad_hidden, weight_grad)
```

```python
import functools
import math

import jax
import jax.numpy as jnp
import numpy as np
from jax import lax
from jax.experimental import pallas as pl
from jax.experimental.pallas import tpu as pltpu
from jax.sharding import PartitionSpec as P

FF = 28672
ROWS = 128
LOCAL = 1792
COLS = 512
LANES = 128
BLOCKS = LOCAL // LANES
N_Z = 8
HALF = 896
CHUNKS = ((0, 512), (512, 896))
BF16 = jnp.bfloat16
F32 = jnp.float32


def _linear(z, x, y, core):
    return ((z % 8) * 2 + x % 2) * 16 + (y % 4) * 4 + (x % 4) // 2 * 2 + core


def _permute(value, move):
    pairs = []
    for z in range(8):
        for x in range(4):
            for y in range(4):
                for core in range(2):
                    target = move(z, x, y, core)
                    if target is not None:
                        pairs.append((_linear(z, x, y, core), _linear(*target)))
    return lax.ppermute(value, ("dp", "tensor"), pairs)


def _along_z(step):
    return lambda z, x, y, core: (z + step, x, y, core)


def _along_y(step):
    return lambda z, x, y, core: (z, x, y + step, core)


def _pair_x(z, x, y, core):
    return z, x ^ 1, y, core


def _far_x(z, x, y, core):
    return z, x + 2, y, core


def _core(z, x, y, core):
    return z, x, y, 1 - core


def _pair_y(z, x, y, core):
    return z, x, y ^ 1, core


def conference():
    modulus = 13
    residues = set(number * number % modulus for number in range(1, modulus))
    table = np.zeros((modulus + 1, modulus + 1), np.int64)
    table[0, 1:] = 1
    table[1:, 0] = 1
    for row in range(modulus):
        for col in range(modulus):
            if row != col:
                table[row + 1, col + 1] = 1 if (col - row) % modulus in residues else -1
    return table


def sylvester(order):
    matrix = np.ones((1, 1))
    doubler = np.array([[1.0, 1.0], [1.0, -1.0]])
    while matrix.shape[0] < order:
        matrix = np.kron(doubler, matrix)
    return matrix


def block_pair():
    inner = sylvester(64)
    first = np.kron(np.array([[1.0, -1.0], [-1.0, -1.0]]), inner)
    second = np.kron(np.array([[1.0, 1.0], [1.0, -1.0]]), inner)
    return np.concatenate([first, second], axis=1)


SCALE = 1.0 / math.sqrt(FF)


def after(value, *earlier):
    return lax.optimization_barrier((value, earlier))[0]


def _cost(flops, moved):
    return pl.CostEstimate(flops=flops, bytes_accessed=moved, transcendentals=0)


SIDE, SIGN, PLACE = 0, 2, 6
TURNS = ((0, (0, 2, 1, -1)), (1, (0, 2, 1, -1)), (3, (0, 2, 1, -1)), (2, (0, 2)), (2, (1, -1)))


def place_table():
    table = np.zeros((256, 40), np.int32)
    for z in range(8):
        for x in range(4):
            for y in range(4):
                for core in range(2):
                    row = [x % 2, 1 - x % 2]
                    position = y * 4 + x // 2 * 2 + core
                    row += [1 - 2 * (position >> level & 1) for level in range(4)]
                    for number in (core, 1 - core):
                        for turn, steps in TURNS:
                            for step in steps:
                                other_z = 2 * ((y + turn) % 4) + (x + step) % 4 // 2
                                row.append((other_z - z) % 8 * 2 + (number + x) % 2)
                    table[_linear(z, x, y, core), : len(row)] = row
    return table


def _smem():
    return [pl.BlockSpec(memory_space=pltpu.SMEM)]


def _vmem(count):
    return [pl.BlockSpec(memory_space=pltpu.VMEM)] * count


def _params(mebibytes=10):
    return pltpu.CompilerParams(vmem_limit_bytes=mebibytes * 2**20)


def _signed_sums(parts, own, store):
    table = conference()
    for col in range(BLOCKS):
        total = own[col]
        for row in range(BLOCKS):
            if table[row, col] > 0:
                total = total + parts[row]
            elif table[row, col] < 0:
                total = total - parts[row]
        store(col, total * SCALE)


def _first_kernel(place_ref, x_ref, table_ref, weight_ref, out_ref, own_ref, other_ref, first, second, sems):
    copies = []
    for n, ref in enumerate((own_ref, other_ref)):
        row = pl.multiple_of(place_ref[SIDE + n] * HALF, HALF)
        copies.append(pltpu.make_async_copy(weight_ref.at[pl.ds(row, HALF), :], ref, sems.at[n]))
    for copy in copies:
        copy.start()
    for block in range(BLOCKS):
        both = lax.dot_general(
            table_ref[...],
            x_ref[:, block * LANES : (block + 1) * LANES],
            (((0,), (1,)), ((), ())),
            preferred_element_type=F32,
        )
        first[block] = both[:LANES]
        second[block] = both[LANES:]

    def body(step, carry):
        rows = pl.ds(pl.multiple_of(step * 16, 16), 16)
        parts = [first[block, rows, :] for block in range(BLOCKS)]
        own = [second[block, rows, :] for block in range(BLOCKS)]

        def store(col, total):
            out_ref[pl.ds(pl.multiple_of(col * LANES + step * 16, 16), 16), :] = total.astype(BF16)

        _signed_sums(parts, own, store)
        return carry

    lax.fori_loop(0, LANES // 16, body, 0)
    for copy in copies:
        copy.wait()


def first_kernel(place, hidden, table, weight):
    any_space = pl.BlockSpec(memory_space=pl.ANY)
    return pl.pallas_call(
        _first_kernel,
        out_shape=[jax.ShapeDtypeStruct((LOCAL, ROWS), BF16)] + [jax.ShapeDtypeStruct((HALF, COLS), BF16)] * 2,
        in_specs=[pl.BlockSpec(memory_space=pltpu.SMEM)] + _vmem(2) + [any_space],
        out_specs=_vmem(1) + [any_space] * 2,
        scratch_shapes=[pltpu.VMEM((BLOCKS, LANES, ROWS), F32)] * 2 + [pltpu.SemaphoreType.DMA((2,))],
        compiler_params=_params(),
        cost_estimate=_cost(2 * ROWS * LOCAL * 256, 6 * 2**20),
        name="rotate_hidden",
    )(place, hidden, table, weight)


def _level_kernel(level, cut, place_ref, *refs):
    sign = place_ref[SIGN + level].astype(F32)

    def turned(own_ref, partner_ref, rows):
        return (partner_ref[rows, :].astype(F32) + sign * own_ref[rows, :].astype(F32)).astype(BF16)

    if cut == "join":
        half = refs[0].shape[0]
        for n in range(2):
            refs[4][n * half : (n + 1) * half] = turned(refs[n], refs[2 + n], slice(0, half))
    elif cut is None:
        refs[2][...] = turned(refs[0], refs[1], slice(None))
    else:
        half = refs[2].shape[0]
        for n in range(2):
            base = place_ref[SIDE + n] * half if cut == "side" else n * half
            refs[2 + n][...] = turned(refs[0], refs[1], pl.ds(pl.multiple_of(base, half), half))


def level_kernel(place, level, *states, cut=None):
    rows, cols = states[0].shape
    shapes = {None: [rows], "join": [2 * rows]}.get(cut, [rows // 2] * 2)
    out = pl.pallas_call(
        functools.partial(_level_kernel, level, cut),
        out_shape=[jax.ShapeDtypeStruct((r, cols), BF16) for r in shapes],
        in_specs=_smem() + _vmem(len(states)),
        out_specs=_vmem(len(shapes)),
        compiler_params=_params(1),
        cost_estimate=_cost(0, 2**20),
        name="walsh_level",
    )(place, *states)
    return out if len(out) > 1 else out[0]


def _rotate_masked_kernel(place_ref, own_ref, up_ref, down_ref, far_ref, mask_ref, table_ref, out_ref, whole, first, second):
    near = pl.ds(pl.multiple_of(place_ref[SIDE] * HALF, LANES), HALF)
    far = pl.ds(pl.multiple_of(place_ref[SIDE + 1] * HALF, LANES), HALF)
    whole[:, near] = (
        own_ref[:ROWS].astype(F32) + up_ref[:ROWS].astype(F32) + down_ref[:ROWS].astype(F32)
    ).astype(BF16)
    whole[:, far] = far_ref[...]
    for block in range(BLOCKS):
        cols = slice(block * LANES, (block + 1) * LANES)
        kept = jnp.where(mask_ref[:, cols] > 0, whole[:, cols].astype(F32), 0.0).astype(BF16)
        both = jnp.dot(kept, table_ref[...], preferred_element_type=F32)
        first[block] = both[:, :LANES]
        second[block] = both[:, LANES:]

    def body(step, carry):
        rows = pl.ds(pl.multiple_of(step * 16, 16), 16)
        parts = [first[block, rows, :] for block in range(BLOCKS)]
        own = [second[block, rows, :] for block in range(BLOCKS)]

        def store(col, total):
            out_ref[rows, col * LANES : (col + 1) * LANES] = total.astype(BF16)

        _signed_sums(parts, own, store)
        return carry

    lax.fori_loop(0, ROWS // 16, body, 0)


def rotate_masked(place, own, up, down, far, mask, table):
    return pl.pallas_call(
        _rotate_masked_kernel,
        out_shape=jax.ShapeDtypeStruct((ROWS, LOCAL), BF16),
        in_specs=[pl.BlockSpec(memory_space=pltpu.SMEM)] + _vmem(6),
        out_specs=_vmem(1)[0],
        scratch_shapes=[pltpu.VMEM((ROWS, LOCAL), BF16)] + [pltpu.VMEM((BLOCKS, ROWS, LANES), F32)] * 2,
        compiler_params=_params(4),
        cost_estimate=_cost(2 * ROWS * LOCAL * 256, 3 * 2**20),
        name="rotate_masked",
    )(place, own, up, down, far, mask, table)


MOVES = {0: _core, 1: _far_x, 2: _pair_y, 3: _along_y(2)}


def butterfly(place, state, level, *earlier, cut=None):
    partner = _permute(state, MOVES[level])
    return level_kernel(place, level, state, after(partner, *earlier) if earlier else partner, cut=cut)


def _assemble_kernel(place_ref, *refs):
    ins, out_ref, sems = refs[:-2], refs[-2], refs[-1]
    copies = []
    for ref, columns in zip(ins, SOURCE_COLUMNS * 2):
        for n, col in enumerate(columns):
            row = pl.multiple_of(place_ref[PLACE + len(copies)] * ROWS, ROWS)
            copies.append(
                pltpu.make_async_copy(
                    ref.at[pl.ds(n * ROWS, ROWS), :],
                    out_ref.at[pl.ds(row, ROWS), pl.ds(col * COLS, COLS)],
                    sems.at[len(copies)],
                )
            )
    for copy in copies:
        copy.start()
    for copy in copies:
        copy.wait()


def assemble(place, sources):
    return pl.pallas_call(
        _assemble_kernel,
        out_shape=jax.ShapeDtypeStruct((2 * N_Z * ROWS, 2 * COLS), BF16),
        in_specs=[pl.BlockSpec(memory_space=pltpu.SMEM)] + [pl.BlockSpec(memory_space=pl.ANY)] * len(sources),
        out_specs=pl.BlockSpec(memory_space=pl.ANY),
        scratch_shapes=[pltpu.SemaphoreType.DMA((32,))],
        compiler_params=_params(1),
        cost_estimate=_cost(0, 8 * 2**20),
        name="assemble_grad",
    )(place, *sources)


def _partial_kernel(steps, grad_ref, mine_ref, other_ref, *refs):
    outs, weight = refs[:-1], refs[-1]
    weight[:, :COLS] = mine_ref[...]
    weight[:, COLS:] = other_ref[...]
    place = 0
    for step in steps:
        rows = slice(step * 256, step * 256 + 256)
        total = lax.dot_general(
            grad_ref[rows], weight[...], (((1,), (1,)), ((), ())), preferred_element_type=F32
        ).astype(BF16)
        if step == 4:
            outs[place][...] = total[:ROWS]
            outs[place + 1][...] = total[ROWS:]
            place += 2
        else:
            outs[place][...] = total
            place += 1


def partial_products(grad, mine, other, steps):
    rows = sum([[ROWS, ROWS] if step == 4 else [2 * ROWS] for step in steps], [])
    return pl.pallas_call(
        functools.partial(_partial_kernel, steps),
        out_shape=[jax.ShapeDtypeStruct((r, HALF), BF16) for r in rows],
        in_specs=_vmem(3),
        out_specs=_vmem(len(rows)),
        scratch_shapes=[pltpu.VMEM((HALF, 2 * COLS), BF16)],
        compiler_params=_params(5),
        cost_estimate=_cost(4 * 256 * len(steps) * COLS * HALF, 6 * 2**20),
        name="partial_products",
    )(grad, mine, other)


def scatter_ring(pieces, *earlier):
    four_up, four_down, three, five, two, six, one, seven, own = pieces
    forth, back = _along_z(1), _along_z(-1)
    half = ROWS

    def plus(held, arrived):
        return (held.astype(F32) + arrived.astype(F32)).astype(BF16)

    up = _permute(four_up, forth)
    down = _permute(four_down, back)
    up = _permute(jnp.concatenate([plus(three[:half], up), three[half:]], axis=0), forth)
    down = _permute(jnp.concatenate([five[:half], plus(five[half:], down)], axis=0), back)
    up = _permute(plus(two, up), forth)
    down = _permute(plus(six, down), back)
    up = _permute(after(plus(one, up), *earlier), forth)
    down = _permute(after(plus(seven, down), *earlier), back)
    return own, up, down


def gather_ring(own):
    forth, back = _along_z(1), _along_z(-1)
    half = own.shape[0] // 2
    up, down = own, own
    got, steps = {0: own}, []
    for step in range(1, 4):
        up, down = _permute(up, forth), _permute(down, back)
        got[8 - step], got[step] = up, down
        steps.append((up, down))
    last = [_permute(up[:half], forth), _permute(down[half:], back)]
    return [got[step] for step in (0, 1, 2, 3, 5, 6, 7)] + last, steps


def _weight_kernel(low, high, *refs):
    whole, (upper, lower, grad_ref, keep_ref, send_ref, joined) = refs[:7], refs[7:]
    wide = 2 * ROWS
    for step, ref in zip((0, 1, 2, 3, 5, 6, 7), whole):
        joined[:, step * wide : (step + 1) * wide] = ref[low:high]
    half = upper.shape[0]
    middle = slice(4 * wide, 5 * wide)
    if low < half:
        joined[: min(high, half) - low, middle] = upper[low : min(high, half)]
    if high > half:
        joined[max(low, half) - low :, middle] = lower[max(low, half) - half : high - half]
    tile = 128

    def body(step, carry):
        rows = pl.ds(pl.multiple_of(step * tile, tile), tile)
        total = jnp.dot(joined[rows, :], grad_ref[...], preferred_element_type=F32).astype(BF16)
        keep_ref[rows, :] = total[:, :COLS]
        send_ref[rows, :] = total[:, COLS:]
        return carry

    lax.fori_loop(0, joined.shape[0] // tile, body, 0)


def weight_products(gathered, grad, low, high):
    width = high - low
    return pl.pallas_call(
        functools.partial(_weight_kernel, low, high),
        out_shape=[jax.ShapeDtypeStruct((width, COLS), BF16)] * 2,
        in_specs=_vmem(10),
        out_specs=_vmem(2),
        scratch_shapes=[pltpu.VMEM((width, 2 * N_Z * ROWS), BF16)],
        compiler_params=_params(6),
        cost_estimate=_cost(4 * 2 * N_Z * ROWS * COLS * width, 6 * 2**20),
        name="weight_products",
    )(*gathered, grad)


SOURCE_COLUMNS = ((0, 0, 1, 1), (0, 0, 1, 1), (0, 0, 1, 1), (0, 0), (1, 1))


def gather_local(out_grad, *earlier):
    def from_x(step):
        return _permute(out_grad, lambda z, x, y, core: (z, x - step, y, core))

    row = jnp.concatenate([out_grad, from_x(2), from_x(1), after(from_x(-1), *earlier)], axis=0)
    after_y, before_y = _permute(row, _along_y(-1)), _permute(row, _along_y(1))
    half = 2 * ROWS
    opposite = [_permute(after_y[:half], _along_y(-1)), _permute(before_y[half:], _along_y(1))]
    return [row, after_y, before_y] + opposite


def _join_kernel(place_ref, *refs):
    count = 2 * len(CHUNKS)
    ins, out_ref, sems = refs[:count], refs[count], refs[count + 1]
    copies = []
    for n in range(2):
        for (a, b), ref in zip(CHUNKS, ins[n * len(CHUNKS) : (n + 1) * len(CHUNKS)]):
            row = pl.multiple_of(place_ref[SIDE + n] * HALF + a, LANES)
            copies.append(pltpu.make_async_copy(ref, out_ref.at[pl.ds(row, b - a), :], sems.at[len(copies)]))
    for copy in copies:
        copy.start()
    for copy in copies:
        copy.wait()


def join_sides(place, kept, arrived):
    return pl.pallas_call(
        _join_kernel,
        out_shape=jax.ShapeDtypeStruct((LOCAL, COLS), BF16),
        in_specs=_smem() + _vmem(2 * len(CHUNKS)),
        out_specs=pl.BlockSpec(memory_space=pl.ANY),
        scratch_shapes=[pltpu.SemaphoreType.DMA((2 * len(CHUNKS),))],
        compiler_params=_params(1),
        cost_estimate=_cost(0, 4 * 2**20),
        name="join_sides",
    )(place, *kept, *arrived)


def per_device(hidden, out_grad, down_weight, clip_mask):
    place = lax.dynamic_index_in_dim(
        jnp.asarray(place_table()), lax.axis_index(("dp", "tensor")), keepdims=False
    )
    place, out_grad, hidden = lax.optimization_barrier((place, out_grad, hidden))
    table = jnp.asarray(block_pair(), BF16)

    part, weight_own, weight_send = first_kernel(place, hidden, table, down_weight)
    local = gather_local(out_grad, part)
    weight_other = _permute(weight_send, _pair_x)
    part = butterfly(place, part, 0)
    part = butterfly(place, part, 1)
    partner = _permute(after(part, *local), MOVES[2])

    grad = assemble(place, local + [_permute(block, _core) for block in local])
    pieces = partial_products(grad, weight_own, weight_other, (4, 3, 5))
    part = level_kernel(place, 2, part, after(partner, *pieces))
    near, far = butterfly(place, part, 3, cut="side")
    rotated = jnp.concatenate([near, _permute(far, _pair_x)], axis=1)
    gathered, steps = gather_ring(rotated)

    pieces += partial_products(grad, weight_own, weight_other, (2, 6, 1, 7, 0))
    own, up, down = scatter_ring(pieces, rotated)
    swapped = (own[ROWS:].astype(F32) + up[ROWS:].astype(F32) + down[ROWS:].astype(F32)).astype(BF16)
    far = after(_permute(swapped, _pair_x), *steps[1])
    turned_grad = rotate_masked(place, own, up, down, far, clip_mask, table)
    upper, lower = butterfly(place, turned_grad, 0, cut="rows")
    upper, lower = butterfly(place, upper, 2, *steps[2]), butterfly(place, lower, 1, *steps[2])
    upper, lower = butterfly(place, upper, 1, *gathered[7:]), butterfly(place, lower, 2, *gathered[7:])
    partners = [_permute(half, MOVES[3]) for half in (upper, lower)]
    grad_hidden = level_kernel(place, 3, upper, lower, *partners, cut="join")

    kept, arrived = [], []
    for a, b in CHUNKS:
        keep, send = weight_products(gathered, grad, a, b)
        kept.append(keep)
        arrived.append(_permute(send, _pair_x))
    return grad_hidden, join_sides(place, kept, arrived)


def solution(mesh):
    return jax.shard_map(
        per_device,
        mesh=mesh,
        in_specs=(P("dp", "tensor"), P("tensor", "dp"), P("tensor", "dp"), P("dp", "tensor")),
        out_specs=(P("dp", "tensor"), P("tensor", "dp")),
        check_vma=False,
    )
```

```python
import functools
import math

import jax
import jax.numpy as jnp
import numpy as np
from jax import lax
from jax.experimental import pallas as pl
from jax.experimental.pallas import tpu as pltpu
from jax.sharding import PartitionSpec as P

FF = 28672
ROWS = 128
LOCAL = 1792
COLS = 512
LANES = 128
BLOCKS = LOCAL // LANES
N_Z = 8
HALF = 896
CHUNKS = ((0, 512), (512, 896))
BF16 = jnp.bfloat16
F32 = jnp.float32


def _linear(z, x, y, core):
    return ((z % 8) * 2 + x % 2) * 16 + (y % 4) * 4 + (x % 4) // 2 * 2 + core


def _permute(value, move):
    pairs = []
    for z in range(8):
        for x in range(4):
            for y in range(4):
                for core in range(2):
                    target = move(z, x, y, core)
                    if target is not None:
                        pairs.append((_linear(z, x, y, core), _linear(*target)))
    return lax.ppermute(value, ("dp", "tensor"), pairs)


def _along_z(step):
    return lambda z, x, y, core: (z + step, x, y, core)


def _along_y(step):
    return lambda z, x, y, core: (z, x, y + step, core)


def _pair_x(z, x, y, core):
    return z, x ^ 1, y, core


def _far_x(z, x, y, core):
    return z, x + 2, y, core


def _core(z, x, y, core):
    return z, x, y, 1 - core


def _pair_y(z, x, y, core):
    return z, x, y ^ 1, core


def conference():
    modulus = 13
    residues = set(number * number % modulus for number in range(1, modulus))
    table = np.zeros((modulus + 1, modulus + 1), np.int64)
    table[0, 1:] = 1
    table[1:, 0] = 1
    for row in range(modulus):
        for col in range(modulus):
            if row != col:
                table[row + 1, col + 1] = 1 if (col - row) % modulus in residues else -1
    return table


def sylvester(order):
    matrix = np.ones((1, 1))
    doubler = np.array([[1.0, 1.0], [1.0, -1.0]])
    while matrix.shape[0] < order:
        matrix = np.kron(doubler, matrix)
    return matrix


def block_pair():
    inner = sylvester(64)
    first = np.kron(np.array([[1.0, -1.0], [-1.0, -1.0]]), inner)
    second = np.kron(np.array([[1.0, 1.0], [1.0, -1.0]]), inner)
    return np.concatenate([first, second], axis=1)


SCALE = 1.0 / math.sqrt(FF)


def after(value, *earlier):
    return lax.optimization_barrier((value, earlier))[0]


def _cost(flops, moved):
    return pl.CostEstimate(flops=flops, bytes_accessed=moved, transcendentals=0)


SIDE, SIGN, PLACE, QUARTER, MIX = 0, 2, 6, 38, 46
TURNS = ((0, (0, 2, 1, -1)), (1, (0, 2, 1, -1)), (3, (0, 2, 1, -1)), (2, (0, 2)), (2, (1, -1)))


def place_table():
    table = np.zeros((256, 64), np.int32)
    for z in range(8):
        for x in range(4):
            for y in range(4):
                for core in range(2):
                    row = [x % 2, 1 - x % 2]
                    position = y * 4 + x // 2 * 2 + core
                    row += [1 - 2 * (position >> level & 1) for level in range(4)]
                    for number in (core, 1 - core):
                        for turn, steps in TURNS:
                            for step in steps:
                                other_z = 2 * ((y + turn) % 4) + (x + step) % 4 // 2
                                row.append((other_z - z) % 8 * 2 + (number + x) % 2)
                    row += [(y + k) % 4 for k in range(4)] + [(y - k) % 4 for k in range(4)]
                    row += [(-1) ** bin((y + k) % 4 & (y - m) % 4).count("1") for k in range(4) for m in range(4)]
                    table[_linear(z, x, y, core), : len(row)] = row
    return table


def _smem():
    return [pl.BlockSpec(memory_space=pltpu.SMEM)]


def _vmem(count):
    return [pl.BlockSpec(memory_space=pltpu.VMEM)] * count


def _params(mebibytes=10):
    return pltpu.CompilerParams(vmem_limit_bytes=mebibytes * 2**20)


def _signed_sums(parts, own, store):
    table = conference()
    for col in range(BLOCKS):
        total = own[col]
        for row in range(BLOCKS):
            if table[row, col] > 0:
                total = total + parts[row]
            elif table[row, col] < 0:
                total = total - parts[row]
        store(col, total * SCALE)


def _weight_rows_kernel(place_ref, weight_ref, own_ref, other_ref):
    for n, ref in enumerate((own_ref, other_ref)):
        ref[...] = weight_ref[pl.ds(pl.multiple_of(place_ref[SIDE + n] * HALF, HALF), HALF), :]


def weight_rows(place, weight):
    return pl.pallas_call(
        _weight_rows_kernel,
        out_shape=[jax.ShapeDtypeStruct((HALF, COLS), BF16)] * 2,
        in_specs=_smem() + _vmem(1),
        out_specs=_vmem(2),
        compiler_params=_params(1),
        cost_estimate=_cost(0, 4 * 2**20),
        name="weight_rows",
    )(place, weight)


def _rotate_kernel(x_ref, table_ref, out_ref, first, second):
    for block in range(BLOCKS):
        both = lax.dot_general(
            table_ref[...],
            x_ref[:, block * LANES : (block + 1) * LANES],
            (((0,), (1,)), ((), ())),
            preferred_element_type=F32,
        )
        first[block] = both[:LANES]
        second[block] = both[LANES:]

    def body(step, carry):
        rows = pl.ds(pl.multiple_of(step * 16, 16), 16)
        parts = [first[block, rows, :] for block in range(BLOCKS)]
        own = [second[block, rows, :] for block in range(BLOCKS)]

        def store(col, total):
            out_ref[pl.ds(pl.multiple_of(col * LANES + step * 16, 16), 16), :] = total.astype(BF16)

        _signed_sums(parts, own, store)
        return carry

    lax.fori_loop(0, LANES // 16, body, 0)


def rotate_hidden(hidden, table):
    return pl.pallas_call(
        _rotate_kernel,
        out_shape=jax.ShapeDtypeStruct((LOCAL, ROWS), BF16),
        in_specs=_vmem(2),
        out_specs=_vmem(1)[0],
        scratch_shapes=[pltpu.VMEM((BLOCKS, LANES, ROWS), F32)] * 2,
        compiler_params=_params(4),
        cost_estimate=_cost(2 * ROWS * LOCAL * 256, 2**20),
        name="rotate_hidden",
    )(hidden, table)


def _level_kernel(level, cut, place_ref, *refs):
    sign = place_ref[SIGN + level].astype(F32)

    def turned(own_ref, partner_ref, rows):
        return (partner_ref[rows, :].astype(F32) + sign * own_ref[rows, :].astype(F32)).astype(BF16)

    if cut == "join":
        half = refs[0].shape[0]
        for n in range(2):
            refs[4][n * half : (n + 1) * half] = turned(refs[n], refs[2 + n], slice(0, half))
    elif cut is None:
        refs[2][...] = turned(refs[0], refs[1], slice(None))
    elif cut == "quarters":
        part = refs[2].shape[0]
        for n in range(4):
            rows = pl.ds(pl.multiple_of(place_ref[QUARTER + n] * part, part), part)
            refs[2 + n][...] = turned(refs[0], refs[1], rows)
    else:
        half = refs[2].shape[0]
        for n in range(2):
            base = place_ref[SIDE + n] * half if cut == "side" else n * half
            refs[2 + n][...] = turned(refs[0], refs[1], pl.ds(pl.multiple_of(base, half), half))


def level_kernel(place, level, *states, cut=None):
    rows, cols = states[0].shape
    shapes = {None: [rows], "join": [2 * rows], "quarters": [rows // 4] * 4}.get(cut, [rows // 2] * 2)
    out = pl.pallas_call(
        functools.partial(_level_kernel, level, cut),
        out_shape=[jax.ShapeDtypeStruct((r, cols), BF16) for r in shapes],
        in_specs=_smem() + _vmem(len(states)),
        out_specs=_vmem(len(shapes)),
        compiler_params=_params(1),
        cost_estimate=_cost(0, 2**20),
        name="walsh_level",
    )(place, *states)
    return out if len(out) > 1 else out[0]


def _mix_kernel(place_ref, *refs):
    states = [ref[...].astype(F32) for ref in refs[:4]]
    for k in range(4):
        total = 0.0
        for m in range(4):
            total = total + place_ref[MIX + 4 * k + m].astype(F32) * states[m]
        refs[4 + k][...] = total.astype(BF16)


def mix_kernel(place, states):
    return pl.pallas_call(
        _mix_kernel,
        out_shape=[jax.ShapeDtypeStruct(states[0].shape, BF16)] * 4,
        in_specs=_smem() + _vmem(4),
        out_specs=_vmem(4),
        compiler_params=_params(2),
        cost_estimate=_cost(0, 2**20),
        name="mix_y",
    )(place, *states)


def _join_quarters_kernel(sides, place_ref, *refs):
    part = refs[0].shape[0]
    whole = refs[-1]
    for k in range(4):
        rows = pl.ds(pl.multiple_of(place_ref[QUARTER + 4 + k] * part, part), part)
        whole[rows, :] = refs[k][...]
    if sides:
        for n in range(2):
            rows = pl.ds(pl.multiple_of(place_ref[SIDE + n] * 2 * part, 2 * part), 2 * part)
            refs[4 + n][...] = whole[rows, :]


def join_quarters(place, states, sides=False):
    rows, cols = states[0].shape
    count, height = (2, 2 * rows) if sides else (1, 4 * rows)
    out = pl.pallas_call(
        functools.partial(_join_quarters_kernel, sides),
        out_shape=[jax.ShapeDtypeStruct((height, cols), BF16)] * count,
        in_specs=_smem() + _vmem(4),
        out_specs=_vmem(count),
        scratch_shapes=[pltpu.VMEM((4 * rows, cols), BF16)] if sides else [],
        compiler_params=_params(2),
        cost_estimate=_cost(0, 2**20),
        name="join_quarters",
    )(place, *states)
    return out if sides else out[0]


def shift_y(states, *earlier):
    own, rest = states[0], states[1:]
    rest = after(rest, *earlier) if earlier else rest
    return [own] + [_permute(state, _along_y(k)) for k, state in enumerate(rest, 1)]


def _rotate_masked_kernel(place_ref, own_ref, up_ref, down_ref, far_ref, mask_ref, table_ref, out_ref, whole, first, second):
    near = pl.ds(pl.multiple_of(place_ref[SIDE] * HALF, LANES), HALF)
    far = pl.ds(pl.multiple_of(place_ref[SIDE + 1] * HALF, LANES), HALF)
    whole[:, near] = (
        own_ref[:ROWS].astype(F32) + up_ref[:ROWS].astype(F32) + down_ref[:ROWS].astype(F32)
    ).astype(BF16)
    whole[:, far] = far_ref[...]
    for block in range(BLOCKS):
        cols = slice(block * LANES, (block + 1) * LANES)
        kept = jnp.where(mask_ref[:, cols] > 0, whole[:, cols].astype(F32), 0.0).astype(BF16)
        both = jnp.dot(kept, table_ref[...], preferred_element_type=F32)
        first[block] = both[:, :LANES]
        second[block] = both[:, LANES:]

    def body(step, carry):
        rows = pl.ds(pl.multiple_of(step * 16, 16), 16)
        parts = [first[block, rows, :] for block in range(BLOCKS)]
        own = [second[block, rows, :] for block in range(BLOCKS)]

        def store(col, total):
            out_ref[rows, col * LANES : (col + 1) * LANES] = total.astype(BF16)

        _signed_sums(parts, own, store)
        return carry

    lax.fori_loop(0, ROWS // 16, body, 0)


def rotate_masked(place, own, up, down, far, mask, table):
    return pl.pallas_call(
        _rotate_masked_kernel,
        out_shape=jax.ShapeDtypeStruct((ROWS, LOCAL), BF16),
        in_specs=[pl.BlockSpec(memory_space=pltpu.SMEM)] + _vmem(6),
        out_specs=_vmem(1)[0],
        scratch_shapes=[pltpu.VMEM((ROWS, LOCAL), BF16)] + [pltpu.VMEM((BLOCKS, ROWS, LANES), F32)] * 2,
        compiler_params=_params(4),
        cost_estimate=_cost(2 * ROWS * LOCAL * 256, 3 * 2**20),
        name="rotate_masked",
    )(place, own, up, down, far, mask, table)


MOVES = {0: _core, 1: _far_x, 2: _pair_y, 3: _along_y(2)}


def butterfly(place, state, level, *earlier, cut=None):
    partner = _permute(state, MOVES[level])
    return level_kernel(place, level, state, after(partner, *earlier) if earlier else partner, cut=cut)


def _assemble_kernel(place_ref, *refs):
    ins, out_ref, sems = refs[:-2], refs[-2], refs[-1]
    copies = []
    for ref, columns in zip(ins, SOURCE_COLUMNS * 2):
        for n, col in enumerate(columns):
            row = pl.multiple_of(place_ref[PLACE + len(copies)] * ROWS, ROWS)
            copies.append(
                pltpu.make_async_copy(
                    ref.at[pl.ds(n * ROWS, ROWS), :],
                    out_ref.at[pl.ds(row, ROWS), pl.ds(col * COLS, COLS)],
                    sems.at[len(copies)],
                )
            )
    for copy in copies:
        copy.start()
    for copy in copies:
        copy.wait()


def assemble(place, sources):
    return pl.pallas_call(
        _assemble_kernel,
        out_shape=jax.ShapeDtypeStruct((2 * N_Z * ROWS, 2 * COLS), BF16),
        in_specs=[pl.BlockSpec(memory_space=pltpu.SMEM)] + [pl.BlockSpec(memory_space=pl.ANY)] * len(sources),
        out_specs=pl.BlockSpec(memory_space=pl.ANY),
        scratch_shapes=[pltpu.SemaphoreType.DMA((32,))],
        compiler_params=_params(1),
        cost_estimate=_cost(0, 8 * 2**20),
        name="assemble_grad",
    )(place, *sources)


def _partial_kernel(steps, grad_ref, mine_ref, other_ref, *refs):
    outs, weight = refs[:-1], refs[-1]
    weight[:, :COLS] = mine_ref[...]
    weight[:, COLS:] = other_ref[...]
    place = 0
    for step in steps:
        rows = slice(step * 256, step * 256 + 256)
        total = lax.dot_general(
            grad_ref[rows], weight[...], (((1,), (1,)), ((), ())), preferred_element_type=F32
        ).astype(BF16)
        if step == 4:
            outs[place][...] = total[:ROWS]
            outs[place + 1][...] = total[ROWS:]
            place += 2
        else:
            outs[place][...] = total
            place += 1


def partial_products(grad, mine, other, steps):
    rows = sum([[ROWS, ROWS] if step == 4 else [2 * ROWS] for step in steps], [])
    return pl.pallas_call(
        functools.partial(_partial_kernel, steps),
        out_shape=[jax.ShapeDtypeStruct((r, HALF), BF16) for r in rows],
        in_specs=_vmem(3),
        out_specs=_vmem(len(rows)),
        scratch_shapes=[pltpu.VMEM((HALF, 2 * COLS), BF16)],
        compiler_params=_params(5),
        cost_estimate=_cost(4 * 256 * len(steps) * COLS * HALF, 6 * 2**20),
        name="partial_products",
    )(grad, mine, other)


def scatter_ring(pieces):
    four_up, four_down, three, five, two, six, one, seven, own = pieces
    forth, back = _along_z(1), _along_z(-1)
    half = ROWS

    def plus(held, arrived):
        return (held.astype(F32) + arrived.astype(F32)).astype(BF16)

    up = _permute(four_up, forth)
    down = _permute(four_down, back)
    sent = [
        (
            jnp.concatenate([plus(three[:half], up), three[half:]], axis=0),
            jnp.concatenate([five[:half], plus(five[half:], down)], axis=0),
        )
    ]
    for above, below in ((two, six), (one, seven)):
        up, down = _permute(sent[-1][0], forth), _permute(sent[-1][1], back)
        sent.append((plus(above, up), plus(below, down)))
    return (own, _permute(sent[-1][0], forth), _permute(sent[-1][1], back)), sent


def gather_ring(own):
    forth, back = _along_z(1), _along_z(-1)
    half = own.shape[0] // 2
    up, down = own, own
    got, steps = {0: own}, []
    for step in range(1, 4):
        up, down = _permute(up, forth), _permute(down, back)
        got[8 - step], got[step] = up, down
        steps.append((up, down))
    steps.append((_permute(up[:half], forth), _permute(down[half:], back)))
    return [got[step] for step in (0, 1, 2, 3, 5, 6, 7)] + list(steps[3]), steps


def _weight_kernel(low, high, *refs):
    whole, (upper, lower, grad_ref, keep_ref, send_ref, joined) = refs[:7], refs[7:]
    wide = 2 * ROWS
    for step, ref in zip((0, 1, 2, 3, 5, 6, 7), whole):
        joined[:, step * wide : (step + 1) * wide] = ref[low:high]
    half = upper.shape[0]
    middle = slice(4 * wide, 5 * wide)
    if low < half:
        joined[: min(high, half) - low, middle] = upper[low : min(high, half)]
    if high > half:
        joined[max(low, half) - low :, middle] = lower[max(low, half) - half : high - half]
    tile = 128

    def body(step, carry):
        rows = pl.ds(pl.multiple_of(step * tile, tile), tile)
        total = jnp.dot(joined[rows, :], grad_ref[...], preferred_element_type=F32).astype(BF16)
        keep_ref[rows, :] = total[:, :COLS]
        send_ref[rows, :] = total[:, COLS:]
        return carry

    lax.fori_loop(0, joined.shape[0] // tile, body, 0)


def weight_products(gathered, grad, low, high):
    width = high - low
    return pl.pallas_call(
        functools.partial(_weight_kernel, low, high),
        out_shape=[jax.ShapeDtypeStruct((width, COLS), BF16)] * 2,
        in_specs=_vmem(10),
        out_specs=_vmem(2),
        scratch_shapes=[pltpu.VMEM((width, 2 * N_Z * ROWS), BF16)],
        compiler_params=_params(6),
        cost_estimate=_cost(4 * 2 * N_Z * ROWS * COLS * width, 6 * 2**20),
        name="weight_products",
    )(*gathered, grad)


SOURCE_COLUMNS = ((0, 0, 1, 1), (0, 0, 1, 1), (0, 0, 1, 1), (0, 0), (1, 1))


def gather_local(out_grad, earlier, later):
    def from_x(step):
        return _permute(out_grad, lambda z, x, y, core: (z, x - step, y, core))

    row = jnp.concatenate([out_grad, from_x(2), from_x(1), after(from_x(-1), *earlier)], axis=0)
    after_y, before_y = _permute(row, _along_y(-1)), _permute(row, _along_y(1))
    half = 2 * ROWS
    after_half, before_half = after((after_y[:half], before_y[half:]), later)
    opposite = [_permute(after_half, _along_y(-1)), _permute(before_half, _along_y(1))]
    return [row, after_y, before_y] + opposite


def _join_kernel(place_ref, *refs):
    count = 2 * len(CHUNKS)
    ins, out_ref, sems = refs[:count], refs[count], refs[count + 1]
    copies = []
    for n in range(2):
        for (a, b), ref in zip(CHUNKS, ins[n * len(CHUNKS) : (n + 1) * len(CHUNKS)]):
            row = pl.multiple_of(place_ref[SIDE + n] * HALF + a, LANES)
            copies.append(pltpu.make_async_copy(ref, out_ref.at[pl.ds(row, b - a), :], sems.at[len(copies)]))
    for copy in copies:
        copy.start()
    for copy in copies:
        copy.wait()


def join_sides(place, kept, arrived):
    return pl.pallas_call(
        _join_kernel,
        out_shape=jax.ShapeDtypeStruct((LOCAL, COLS), BF16),
        in_specs=_smem() + _vmem(2 * len(CHUNKS)),
        out_specs=pl.BlockSpec(memory_space=pl.ANY),
        scratch_shapes=[pltpu.SemaphoreType.DMA((2 * len(CHUNKS),))],
        compiler_params=_params(1),
        cost_estimate=_cost(0, 4 * 2**20),
        name="join_sides",
    )(place, *kept, *arrived)


def per_device(hidden, out_grad, down_weight, clip_mask):
    place = lax.dynamic_index_in_dim(
        jnp.asarray(place_table()), lax.axis_index(("dp", "tensor")), keepdims=False
    )
    place, hidden = lax.optimization_barrier((place, hidden))
    table = jnp.asarray(block_pair(), BF16)

    turned = rotate_hidden(hidden, table)
    weight_own, weight_send = weight_rows(place, down_weight)
    weight_other = _permute(weight_send, _pair_x)
    part = butterfly(place, turned, 1)
    part = butterfly(place, part, 0)
    local = gather_local(out_grad, (turned, weight_send), part)
    swapped = [_permute(block, _core) for block in local]

    partner = _permute(after(part, *local), MOVES[2])
    grad = assemble(place, after(local, weight_other) + swapped)
    pieces = partial_products(grad, weight_own, weight_other, (4, 3, 5))
    late = partial_products(grad, weight_own, weight_other, (2, 6, 1, 7, 0))
    (own, up, down), sent = scatter_ring(pieces + late)
    part = level_kernel(place, 2, part, after(partner, *pieces))
    near, far = butterfly(place, part, 3, cut="side")
    rotated = jnp.concatenate([near, _permute(far, _pair_x)], axis=1)
    gathered, steps = gather_ring(rotated)

    swapped = (own[ROWS:].astype(F32) + up[ROWS:].astype(F32) + down[ROWS:].astype(F32)).astype(BF16)
    far = after(_permute(swapped, _pair_x), *steps[1])
    turned_grad = rotate_masked(place, own, up, down, far, clip_mask, table)
    turned_grad = butterfly(place, turned_grad, 1, *steps[3])
    quarters = butterfly(place, turned_grad, 0, cut="quarters")
    quarters = mix_kernel(place, shift_y(quarters))
    grad_hidden = join_quarters(place, shift_y(quarters))

    kept, arrived = [], []
    for a, b in CHUNKS:
        keep, send = weight_products(gathered, grad, a, b)
        kept.append(keep)
        arrived.append(_permute(send, _pair_x))
    return grad_hidden, join_sides(place, kept, arrived)


def solution(mesh):
    return jax.shard_map(
        per_device,
        mesh=mesh,
        in_specs=(P("dp", "tensor"), P("tensor", "dp"), P("tensor", "dp"), P("dp", "tensor")),
        out_specs=(P("dp", "tensor"), P("tensor", "dp")),
        check_vma=False,
    )
```

```python
import functools
import math

import jax
import jax.numpy as jnp
import numpy as np
from jax import lax
from jax.experimental import pallas as pl
from jax.experimental.pallas import tpu as pltpu
from jax.sharding import PartitionSpec as P

FF = 28672
ROWS = 128
LOCAL = 1792
COLS = 512
LANES = 128
BLOCKS = LOCAL // LANES
N_Z = 8
HALF = 896
CHUNKS = ((0, 512), (512, 896))
BF16 = jnp.bfloat16
F32 = jnp.float32


def _linear(z, x, y, core):
    return ((z % 8) * 2 + x % 2) * 16 + (y % 4) * 4 + (x % 4) // 2 * 2 + core


def _permute(value, move):
    pairs = []
    for z in range(8):
        for x in range(4):
            for y in range(4):
                for core in range(2):
                    target = move(z, x, y, core)
                    if target is not None:
                        pairs.append((_linear(z, x, y, core), _linear(*target)))
    return lax.ppermute(value, ("dp", "tensor"), pairs)


def _along_z(step):
    return lambda z, x, y, core: (z + step, x, y, core)


def _along_y(step):
    return lambda z, x, y, core: (z, x, y + step, core)


def _pair_x(z, x, y, core):
    return z, x ^ 1, y, core


def _far_x(z, x, y, core):
    return z, x + 2, y, core


def _core(z, x, y, core):
    return z, x, y, 1 - core


def _pair_y(z, x, y, core):
    return z, x, y ^ 1, core


def conference():
    modulus = 13
    residues = set(number * number % modulus for number in range(1, modulus))
    table = np.zeros((modulus + 1, modulus + 1), np.int64)
    table[0, 1:] = 1
    table[1:, 0] = 1
    for row in range(modulus):
        for col in range(modulus):
            if row != col:
                table[row + 1, col + 1] = 1 if (col - row) % modulus in residues else -1
    return table


def sylvester(order):
    matrix = np.ones((1, 1))
    doubler = np.array([[1.0, 1.0], [1.0, -1.0]])
    while matrix.shape[0] < order:
        matrix = np.kron(doubler, matrix)
    return matrix


def block_pair():
    inner = sylvester(64)
    first = np.kron(np.array([[1.0, -1.0], [-1.0, -1.0]]), inner)
    second = np.kron(np.array([[1.0, 1.0], [1.0, -1.0]]), inner)
    return np.concatenate([first, second], axis=1)


SCALE = 1.0 / math.sqrt(FF)


def after(value, *earlier):
    return lax.optimization_barrier((value, earlier))[0]


def _cost(flops, moved):
    return pl.CostEstimate(flops=flops, bytes_accessed=moved, transcendentals=0)


SIDE, SIGN, PLACE, QUARTER, MIX = 0, 2, 6, 38, 46
TURNS = ((0, (0, 2, 1, -1)), (1, (0, 2, 1, -1)), (3, (0, 2, 1, -1)), (2, (0, 2)), (2, (1, -1)))


def place_table():
    table = np.zeros((256, 64), np.int32)
    for z in range(8):
        for x in range(4):
            for y in range(4):
                for core in range(2):
                    row = [x % 2, 1 - x % 2]
                    position = y * 4 + x // 2 * 2 + core
                    row += [1 - 2 * (position >> level & 1) for level in range(4)]
                    for number in (core, 1 - core):
                        for turn, steps in TURNS:
                            for step in steps:
                                other_z = 2 * ((y + turn) % 4) + (x + step) % 4 // 2
                                row.append((other_z - z) % 8 * 2 + (number + x) % 2)
                    row += [(y + k) % 4 for k in range(4)] + [(y - k) % 4 for k in range(4)]
                    row += [(-1) ** bin((y + k) % 4 & (y - m) % 4).count("1") for k in range(4) for m in range(4)]
                    table[_linear(z, x, y, core), : len(row)] = row
    return table


def _smem():
    return [pl.BlockSpec(memory_space=pltpu.SMEM)]


def _vmem(count):
    return [pl.BlockSpec(memory_space=pltpu.VMEM)] * count


def _params(mebibytes=10):
    return pltpu.CompilerParams(vmem_limit_bytes=mebibytes * 2**20)


def _signed_sums(parts, own, store):
    table = conference()
    for col in range(BLOCKS):
        total = own[col]
        for row in range(BLOCKS):
            if table[row, col] > 0:
                total = total + parts[row]
            elif table[row, col] < 0:
                total = total - parts[row]
        store(col, total * SCALE)


def _weight_rows_kernel(place_ref, weight_ref, own_ref, other_ref):
    for n, ref in enumerate((own_ref, other_ref)):
        ref[...] = weight_ref[pl.ds(pl.multiple_of(place_ref[SIDE + n] * HALF, HALF), HALF), :]


def weight_rows(place, weight):
    return pl.pallas_call(
        _weight_rows_kernel,
        out_shape=[jax.ShapeDtypeStruct((HALF, COLS), BF16)] * 2,
        in_specs=_smem() + _vmem(1),
        out_specs=_vmem(2),
        compiler_params=_params(1),
        cost_estimate=_cost(0, 4 * 2**20),
        name="weight_rows",
    )(place, weight)


def _rotate_kernel(x_ref, table_ref, out_ref, first, second):
    for block in range(BLOCKS):
        both = lax.dot_general(
            table_ref[...],
            x_ref[:, block * LANES : (block + 1) * LANES],
            (((0,), (1,)), ((), ())),
            preferred_element_type=F32,
        )
        first[block] = both[:LANES]
        second[block] = both[LANES:]

    def body(step, carry):
        rows = pl.ds(pl.multiple_of(step * 16, 16), 16)
        parts = [first[block, rows, :] for block in range(BLOCKS)]
        own = [second[block, rows, :] for block in range(BLOCKS)]

        def store(col, total):
            out_ref[pl.ds(pl.multiple_of(col * LANES + step * 16, 16), 16), :] = total.astype(BF16)

        _signed_sums(parts, own, store)
        return carry

    lax.fori_loop(0, LANES // 16, body, 0)


def rotate_hidden(hidden, table):
    return pl.pallas_call(
        _rotate_kernel,
        out_shape=jax.ShapeDtypeStruct((LOCAL, ROWS), BF16),
        in_specs=_vmem(2),
        out_specs=_vmem(1)[0],
        scratch_shapes=[pltpu.VMEM((BLOCKS, LANES, ROWS), F32)] * 2,
        compiler_params=_params(4),
        cost_estimate=_cost(2 * ROWS * LOCAL * 256, 2**20),
        name="rotate_hidden",
    )(hidden, table)


def _level_kernel(level, cut, place_ref, *refs):
    sign = place_ref[SIGN + level].astype(F32)

    def turned(own_ref, partner_ref, rows):
        return (partner_ref[rows, :].astype(F32) + sign * own_ref[rows, :].astype(F32)).astype(BF16)

    if cut == "join":
        half = refs[0].shape[0]
        for n in range(2):
            refs[4][n * half : (n + 1) * half] = turned(refs[n], refs[2 + n], slice(0, half))
    elif cut is None:
        refs[2][...] = turned(refs[0], refs[1], slice(None))
    elif cut == "quarters":
        part = refs[2].shape[0]
        for n in range(4):
            rows = pl.ds(pl.multiple_of(place_ref[QUARTER + n] * part, part), part)
            refs[2 + n][...] = turned(refs[0], refs[1], rows)
    else:
        half = refs[2].shape[0]
        for n in range(2):
            base = place_ref[SIDE + n] * half if cut == "side" else n * half
            refs[2 + n][...] = turned(refs[0], refs[1], pl.ds(pl.multiple_of(base, half), half))


def level_kernel(place, level, *states, cut=None):
    rows, cols = states[0].shape
    shapes = {None: [rows], "join": [2 * rows], "quarters": [rows // 4] * 4}.get(cut, [rows // 2] * 2)
    out = pl.pallas_call(
        functools.partial(_level_kernel, level, cut),
        out_shape=[jax.ShapeDtypeStruct((r, cols), BF16) for r in shapes],
        in_specs=_smem() + _vmem(len(states)),
        out_specs=_vmem(len(shapes)),
        compiler_params=_params(1),
        cost_estimate=_cost(0, 2**20),
        name="walsh_level",
    )(place, *states)
    return out if len(out) > 1 else out[0]


def _mix_kernel(place_ref, *refs):
    states = [ref[...].astype(F32) for ref in refs[:4]]
    for k in range(4):
        total = 0.0
        for m in range(4):
            total = total + place_ref[MIX + 4 * k + m].astype(F32) * states[m]
        refs[4 + k][...] = total.astype(BF16)


def mix_kernel(place, states):
    return pl.pallas_call(
        _mix_kernel,
        out_shape=[jax.ShapeDtypeStruct(states[0].shape, BF16)] * 4,
        in_specs=_smem() + _vmem(4),
        out_specs=_vmem(4),
        compiler_params=_params(2),
        cost_estimate=_cost(0, 2**20),
        name="mix_y",
    )(place, *states)


def _join_quarters_kernel(sides, place_ref, *refs):
    part = refs[0].shape[0]
    whole = refs[-1]
    for k in range(4):
        rows = pl.ds(pl.multiple_of(place_ref[QUARTER + 4 + k] * part, part), part)
        whole[rows, :] = refs[k][...]
    if sides:
        for n in range(2):
            rows = pl.ds(pl.multiple_of(place_ref[SIDE + n] * 2 * part, 2 * part), 2 * part)
            refs[4 + n][...] = whole[rows, :]


def join_quarters(place, states, sides=False):
    rows, cols = states[0].shape
    count, height = (2, 2 * rows) if sides else (1, 4 * rows)
    out = pl.pallas_call(
        functools.partial(_join_quarters_kernel, sides),
        out_shape=[jax.ShapeDtypeStruct((height, cols), BF16)] * count,
        in_specs=_smem() + _vmem(4),
        out_specs=_vmem(count),
        scratch_shapes=[pltpu.VMEM((4 * rows, cols), BF16)] if sides else [],
        compiler_params=_params(2),
        cost_estimate=_cost(0, 2**20),
        name="join_quarters",
    )(place, *states)
    return out if sides else out[0]


def shift_y(states, *earlier):
    own, rest = states[0], states[1:]
    rest = after(rest, *earlier) if earlier else rest
    return [own] + [_permute(state, _along_y(k)) for k, state in enumerate(rest, 1)]


def _rotate_masked_kernel(place_ref, own_ref, up_ref, down_ref, far_ref, mask_ref, table_ref, out_ref, whole, first, second):
    near = pl.ds(pl.multiple_of(place_ref[SIDE] * HALF, LANES), HALF)
    far = pl.ds(pl.multiple_of(place_ref[SIDE + 1] * HALF, LANES), HALF)
    whole[:, near] = (
        own_ref[:ROWS].astype(F32) + up_ref[:ROWS].astype(F32) + down_ref[:ROWS].astype(F32)
    ).astype(BF16)
    whole[:, far] = far_ref[...]
    for block in range(BLOCKS):
        cols = slice(block * LANES, (block + 1) * LANES)
        kept = jnp.where(mask_ref[:, cols] > 0, whole[:, cols].astype(F32), 0.0).astype(BF16)
        both = jnp.dot(kept, table_ref[...], preferred_element_type=F32)
        first[block] = both[:, :LANES]
        second[block] = both[:, LANES:]

    def body(step, carry):
        rows = pl.ds(pl.multiple_of(step * 16, 16), 16)
        parts = [first[block, rows, :] for block in range(BLOCKS)]
        own = [second[block, rows, :] for block in range(BLOCKS)]

        def store(col, total):
            out_ref[rows, col * LANES : (col + 1) * LANES] = total.astype(BF16)

        _signed_sums(parts, own, store)
        return carry

    lax.fori_loop(0, ROWS // 16, body, 0)


def rotate_masked(place, own, up, down, far, mask, table):
    return pl.pallas_call(
        _rotate_masked_kernel,
        out_shape=jax.ShapeDtypeStruct((ROWS, LOCAL), BF16),
        in_specs=[pl.BlockSpec(memory_space=pltpu.SMEM)] + _vmem(6),
        out_specs=_vmem(1)[0],
        scratch_shapes=[pltpu.VMEM((ROWS, LOCAL), BF16)] + [pltpu.VMEM((BLOCKS, ROWS, LANES), F32)] * 2,
        compiler_params=_params(4),
        cost_estimate=_cost(2 * ROWS * LOCAL * 256, 3 * 2**20),
        name="rotate_masked",
    )(place, own, up, down, far, mask, table)


MOVES = {0: _core, 1: _far_x, 2: _pair_y, 3: _along_y(2)}


def butterfly(place, state, level, *earlier, cut=None):
    partner = _permute(state, MOVES[level])
    return level_kernel(place, level, state, after(partner, *earlier) if earlier else partner, cut=cut)


def _assemble_kernel(place_ref, *refs):
    ins, out_ref, sems = refs[:-2], refs[-2], refs[-1]
    copies = []
    for ref, columns in zip(ins, SOURCE_COLUMNS * 2):
        for n, col in enumerate(columns):
            row = pl.multiple_of(place_ref[PLACE + len(copies)] * ROWS, ROWS)
            copies.append(
                pltpu.make_async_copy(
                    ref.at[pl.ds(n * ROWS, ROWS), :],
                    out_ref.at[pl.ds(row, ROWS), pl.ds(col * COLS, COLS)],
                    sems.at[len(copies)],
                )
            )
    for copy in copies:
        copy.start()
    for copy in copies:
        copy.wait()


def assemble(place, sources):
    return pl.pallas_call(
        _assemble_kernel,
        out_shape=jax.ShapeDtypeStruct((2 * N_Z * ROWS, 2 * COLS), BF16),
        in_specs=[pl.BlockSpec(memory_space=pltpu.SMEM)] + [pl.BlockSpec(memory_space=pl.ANY)] * len(sources),
        out_specs=pl.BlockSpec(memory_space=pl.ANY),
        scratch_shapes=[pltpu.SemaphoreType.DMA((32,))],
        compiler_params=_params(1),
        cost_estimate=_cost(0, 8 * 2**20),
        name="assemble_grad",
    )(place, *sources)


def _partial_kernel(steps, grad_ref, mine_ref, other_ref, *refs):
    outs, weight = refs[:-1], refs[-1]
    weight[:, :COLS] = mine_ref[...]
    weight[:, COLS:] = other_ref[...]
    place = 0
    for step in steps:
        rows = slice(step * 256, step * 256 + 256)
        total = lax.dot_general(
            grad_ref[rows], weight[...], (((1,), (1,)), ((), ())), preferred_element_type=F32
        ).astype(BF16)
        if step == 4:
            outs[place][...] = total[:ROWS]
            outs[place + 1][...] = total[ROWS:]
            place += 2
        else:
            outs[place][...] = total
            place += 1


def partial_products(grad, mine, other, steps):
    rows = sum([[ROWS, ROWS] if step == 4 else [2 * ROWS] for step in steps], [])
    return pl.pallas_call(
        functools.partial(_partial_kernel, steps),
        out_shape=[jax.ShapeDtypeStruct((r, HALF), BF16) for r in rows],
        in_specs=_vmem(3),
        out_specs=_vmem(len(rows)),
        scratch_shapes=[pltpu.VMEM((HALF, 2 * COLS), BF16)],
        compiler_params=_params(5),
        cost_estimate=_cost(4 * 256 * len(steps) * COLS * HALF, 6 * 2**20),
        name="partial_products",
    )(grad, mine, other)


def scatter_ring(pieces):
    four_up, four_down, three, five, two, six, one, seven, own = pieces
    forth, back = _along_z(1), _along_z(-1)
    half = ROWS

    def plus(held, arrived):
        return (held.astype(F32) + arrived.astype(F32)).astype(BF16)

    up = _permute(four_up, forth)
    down = _permute(four_down, back)
    sent = [
        (
            jnp.concatenate([plus(three[:half], up), three[half:]], axis=0),
            jnp.concatenate([five[:half], plus(five[half:], down)], axis=0),
        )
    ]
    for above, below in ((two, six), (one, seven)):
        up, down = _permute(sent[-1][0], forth), _permute(sent[-1][1], back)
        sent.append((plus(above, up), plus(below, down)))
    return (own, _permute(sent[-1][0], forth), _permute(sent[-1][1], back)), sent


def gather_ring(own):
    forth, back = _along_z(1), _along_z(-1)
    half = own.shape[0] // 2
    up, down = own, own
    got, steps = {0: own}, []
    for step in range(1, 4):
        up, down = _permute(up, forth), _permute(down, back)
        got[8 - step], got[step] = up, down
        steps.append((up, down))
    steps.append((_permute(up[:half], forth), _permute(down[half:], back)))
    return [got[step] for step in (0, 1, 2, 3, 5, 6, 7)] + list(steps[3]), steps


def _weight_kernel(low, high, *refs):
    whole, (upper, lower, grad_ref, keep_ref, send_ref, joined) = refs[:7], refs[7:]
    wide = 2 * ROWS
    for step, ref in zip((0, 1, 2, 3, 5, 6, 7), whole):
        joined[:, step * wide : (step + 1) * wide] = ref[low:high]
    half = upper.shape[0]
    middle = slice(4 * wide, 5 * wide)
    if low < half:
        joined[: min(high, half) - low, middle] = upper[low : min(high, half)]
    if high > half:
        joined[max(low, half) - low :, middle] = lower[max(low, half) - half : high - half]
    tile = 128

    def body(step, carry):
        rows = pl.ds(pl.multiple_of(step * tile, tile), tile)
        total = jnp.dot(joined[rows, :], grad_ref[...], preferred_element_type=F32).astype(BF16)
        keep_ref[rows, :] = total[:, :COLS]
        send_ref[rows, :] = total[:, COLS:]
        return carry

    lax.fori_loop(0, joined.shape[0] // tile, body, 0)


def weight_products(gathered, grad, low, high):
    width = high - low
    return pl.pallas_call(
        functools.partial(_weight_kernel, low, high),
        out_shape=[jax.ShapeDtypeStruct((width, COLS), BF16)] * 2,
        in_specs=_vmem(10),
        out_specs=_vmem(2),
        scratch_shapes=[pltpu.VMEM((width, 2 * N_Z * ROWS), BF16)],
        compiler_params=_params(6),
        cost_estimate=_cost(4 * 2 * N_Z * ROWS * COLS * width, 6 * 2**20),
        name="weight_products",
    )(*gathered, grad)


SOURCE_COLUMNS = ((0, 0, 1, 1), (0, 0, 1, 1), (0, 0, 1, 1), (0, 0), (1, 1))


def gather_local(out_grad, earlier, later):
    def from_x(step):
        return _permute(out_grad, lambda z, x, y, core: (z, x - step, y, core))

    row = jnp.concatenate([out_grad, from_x(2), from_x(1), after(from_x(-1), *earlier)], axis=0)
    after_y, before_y = _permute(row, _along_y(-1)), _permute(row, _along_y(1))
    half = 2 * ROWS
    after_half, before_half = after((after_y[:half], before_y[half:]), later)
    opposite = [_permute(after_half, _along_y(-1)), _permute(before_half, _along_y(1))]
    return [row, after_y, before_y] + opposite


def _join_kernel(place_ref, *refs):
    count = 2 * len(CHUNKS)
    ins, out_ref, sems = refs[:count], refs[count], refs[count + 1]
    copies = []
    for n in range(2):
        for (a, b), ref in zip(CHUNKS, ins[n * len(CHUNKS) : (n + 1) * len(CHUNKS)]):
            row = pl.multiple_of(place_ref[SIDE + n] * HALF + a, LANES)
            copies.append(pltpu.make_async_copy(ref, out_ref.at[pl.ds(row, b - a), :], sems.at[len(copies)]))
    for copy in copies:
        copy.start()
    for copy in copies:
        copy.wait()


def join_sides(place, kept, arrived):
    return pl.pallas_call(
        _join_kernel,
        out_shape=jax.ShapeDtypeStruct((LOCAL, COLS), BF16),
        in_specs=_smem() + _vmem(2 * len(CHUNKS)),
        out_specs=pl.BlockSpec(memory_space=pl.ANY),
        scratch_shapes=[pltpu.SemaphoreType.DMA((2 * len(CHUNKS),))],
        compiler_params=_params(1),
        cost_estimate=_cost(0, 4 * 2**20),
        name="join_sides",
    )(place, *kept, *arrived)


def per_device(hidden, out_grad, down_weight, clip_mask):
    place = lax.dynamic_index_in_dim(
        jnp.asarray(place_table()), lax.axis_index(("dp", "tensor")), keepdims=False
    )
    place, hidden = lax.optimization_barrier((place, hidden))
    table = jnp.asarray(block_pair(), BF16)

    turned = rotate_hidden(hidden, table)
    weight_own, weight_send = weight_rows(place, down_weight)
    weight_other = _permute(weight_send, _pair_x)
    part = butterfly(place, turned, 1)
    part = butterfly(place, part, 0)
    local = gather_local(out_grad, (turned,), part)
    swapped = [_permute(block, _core) for block in local]

    partner = _permute(after(part, *local), MOVES[2])
    grad = assemble(place, after(local, weight_other) + swapped)
    pieces = partial_products(grad, weight_own, weight_other, (4, 3, 5))
    late = partial_products(grad, weight_own, weight_other, (2, 6, 1, 7, 0))
    (own, up, down), sent = scatter_ring(pieces + late)
    part = level_kernel(place, 2, part, after(partner, *pieces))
    near, far = butterfly(place, part, 3, cut="side")
    rotated = jnp.concatenate([near, _permute(far, _pair_x)], axis=1)
    gathered, steps = gather_ring(rotated)

    swapped = (own[ROWS:].astype(F32) + up[ROWS:].astype(F32) + down[ROWS:].astype(F32)).astype(BF16)
    far = after(_permute(swapped, _pair_x), *steps[1])
    turned_grad = rotate_masked(place, own, up, down, far, clip_mask, table)
    kept, arrived, sends = [], [], []
    for a, b in CHUNKS:
        keep, send = weight_products(gathered, grad, a, b)
        kept.append(keep)
        sends.append(send)
        arrived.append(_permute(send, _pair_x))
    turned_grad = butterfly(place, turned_grad, 1, *steps[3], sends[0])
    quarters = butterfly(place, turned_grad, 0, cut="quarters")
    quarters = mix_kernel(place, shift_y(quarters))
    grad_hidden = join_quarters(place, shift_y(quarters))
    return grad_hidden, join_sides(place, kept, arrived)


def solution(mesh):
    return jax.shard_map(
        per_device,
        mesh=mesh,
        in_specs=(P("dp", "tensor"), P("tensor", "dp"), P("tensor", "dp"), P("dp", "tensor")),
        out_specs=(P("dp", "tensor"), P("tensor", "dp")),
        check_vma=False,
    )
```
